512 devices in a mesh: store: 4 (over x), seq: 16 (over y, core), tp: 8 (over z).
Axes of the slice: x: 4, y: 8, z: 8, core: 2. Of those that a mesh axis runs over, the one named last changes fastest.
Arguments:
- hidden_rows: bfloat16 [16, 128, 8192], P('seq', None, 'store'), may hold values from -6 to 6
- query_weight: bfloat16 [8192, 8, 1024], P('seq', 'tp', 'store'), may hold values from -0.0625 to 0.0625
- kv_weight: bfloat16 [8192, 2048], P('store', 'tp'), may hold values from -0.0625 to 0.0625
- cached_pages: bfloat16 [16, 64, 16, 2048], P('seq', 'store', None, 'tp'), as said below
- page_dest: int32 [16, 64], P('seq', 'store'), may hold values from -1 to 31, as said below
- rec_rows: int32 [16, 128], replicated, may hold values from 0 to 511, as said below
Outputs:
- attended: bfloat16 [16, 128, 8, 1024], P('seq', None, 'tp', 'store')
- blended: bfloat16 [16, 512, 2048], P('seq', 'store', 'tp')
The draws below stay inside these ranges and needn't reach their ends.
Inputs may be any that keep to these rules, and one draw needn't show every extreme that they name: `page_dest`: for each passage every page number 0 to 31 stands in exactly one slot and the other slots hold -1. Slots of one store index hold at most 4 page numbers of one aligned run of 8, and in every passage some store index holds exactly 4 of each run. `rec_rows`: each passage lists 128 distinct rows in rising order, always its first and its last row. `cached_pages`: pages in slots that hold -1 are never read.
All inputs are finite; a program needn't handle non-finite values.
Results may differ from the reference program's by a relative error of at most 0.023.
Values may be sent and summed in bfloat16 or wider, within the bound.
A program may use at most 64 MiB of HBM per device.

```python
import jax
import jax.numpy as jnp
from jax import lax

D = 8192
QH = 64
KVH = 8
HD = 128
PASSAGE = 512
PAGE = 16
REC = 128
PASSAGES = 16
PAGES = 8
CAP = 4
POOL = 16
N_STORE = 4


def permute_pool(slot_key):
    return jax.random.permutation(slot_key, POOL)


def draw_page_dest(key, part):
    key = jax.random.fold_in(key, 11)

    def one_passage(passage_key):
        main_key, other_key, slot_key = jax.random.split(passage_key, 3)
        main_source = jax.random.randint(main_key, (N_STORE,), 0, N_STORE)
        offsets = jax.random.randint(other_key, (N_STORE, PAGES), 1, N_STORE)
        within = jnp.arange(PAGES)[None, :]
        sources = jnp.where(within < CAP, main_source[:, None], (main_source[:, None] + offsets) % N_STORE).reshape(-1)
        page_order = jnp.arange(N_STORE * PAGES, dtype=jnp.int32)
        earlier = (sources[None, :] == sources[:, None]) & (page_order[None, :] < page_order[:, None])
        rank_index = jnp.sum(earlier.astype(jnp.int32), axis=1)
        shuffles = jax.vmap(permute_pool)(jax.random.split(slot_key, N_STORE))
        slot_index = shuffles[sources, rank_index]
        dest_table = jnp.full((N_STORE, POOL), -1, jnp.int32).at[sources, slot_index].set(page_order)
        return dest_table.reshape(-1)
    return jax.vmap(one_passage)(jax.random.split(key, PASSAGES))


def draw_rec_rows(key, part):
    key = jax.random.fold_in(key, 12)

    def one_passage(passage_key):
        middle = jax.random.permutation(passage_key, PASSAGE - 2)[:REC - 2] + 1
        chosen = jnp.concatenate([jnp.array([0, PASSAGE - 1], jnp.int32), middle.astype(jnp.int32)])
        return jnp.sort(chosen)
    return jax.vmap(one_passage)(jax.random.split(key, PASSAGES))


def draw_cached_pages(key, part):
    key = jax.random.fold_in(key, 13)
    value_key = jax.random.fold_in(key, 0)
    full_shape = (PASSAGES, N_STORE * POOL, PAGE, KVH, 2 * HD)
    entries = jax.random.normal(value_key, full_shape, jnp.float32)
    return entries.reshape(PASSAGES, N_STORE * POOL, PAGE, KVH * 2 * HD).astype(jnp.bfloat16)


def level_of(stream_key, dims, cuts, least, high):
    factor_of = 1.0
    for axis_at, blocks in cuts:
        heights = jax.random.uniform(jax.random.fold_in(jax.random.fold_in(stream_key, 6), axis_at), (blocks,), jnp.float32, least / len(cuts), high / len(cuts))
        factor_of = factor_of * jnp.repeat(jnp.exp(heights), dims[axis_at] // blocks).reshape((-1,) + (1,) * (len(dims) - 1 - axis_at))
    return factor_of


def normal_values(own_key, extent, spread, limit, shards=(), kind=jnp.bfloat16):
    values = spread * jax.random.normal(own_key, extent, jnp.float32)
    if shards:
        values = values * level_of(own_key, extent, shards, -0.22, 0.18)
    return jnp.clip(values, -limit, limit).astype(kind)


def setup_inputs(seed: int = 0) -> dict:
    keys = jax.random.split(jax.random.key(seed), 7)
    return {
        "hidden_rows": normal_values(keys[0], (PASSAGES, REC, D), 1.0, 6.0, ((0, 16), (2, 4))),
        "query_weight": normal_values(keys[1], (D, KVH, (QH // KVH) * HD), D ** -0.5, 0.0625, ((0, 16), (1, 8), (2, 4))),
        "kv_weight": normal_values(keys[2], (D, KVH * 2 * HD), D ** -0.5, 0.0625, ((0, 4), (1, 8))),
        "cached_pages": draw_cached_pages(jax.random.fold_in(keys[6], 71), 0),
        "page_dest": draw_page_dest(jax.random.fold_in(keys[6], 71), 0),
        "rec_rows": draw_rec_rows(jax.random.fold_in(keys[6], 71), 0),
    }


rope_base = 500000.0
masked_score = -1e30


def rotate(values, places):
    half_width = values.shape[-1] // 2
    frequency = rope_base ** (-(jnp.arange(half_width, dtype=jnp.float32) * 2.0 / values.shape[-1]))
    angles = places.astype(jnp.float32)[:, None] * frequency[None, :]
    cosine = jnp.cos(angles)[:, None, :]
    sine_part = jnp.sin(angles)[:, None, :]
    first_half = values[..., :half_width]
    second = values[..., half_width:]
    return jnp.concatenate([first_half * cosine - second * sine_part, second * cosine + first_half * sine_part], axis=-1)


def assemble(page_block, targets, fresh_block, chosen):
    page_count = PASSAGE // PAGE
    slot_index = jnp.where(targets >= 0, targets, page_count)
    reused = jnp.zeros((page_count, PAGE, page_block.shape[-1]), jnp.bfloat16)
    reused = reused.at[slot_index].set(page_block, mode="drop").reshape(PASSAGE, page_block.shape[-1])
    return reused.at[chosen].set(fresh_block)


def reference(hidden_rows, query_weight, kv_weight, cached_pages, page_dest, rec_rows):
    group_size = QH // KVH
    passage_ids = jnp.arange(PASSAGES, dtype=jnp.int32)
    places = passage_ids[:, None] * PASSAGE + rec_rows
    flat_places = places.reshape(-1)
    flat_rows = hidden_rows.reshape(PASSAGES * REC, D)
    fresh_rows = jnp.dot(flat_rows, kv_weight, preferred_element_type=jnp.float32).reshape(PASSAGES * REC, KVH, 2 * HD)
    fresh_keys = rotate(fresh_rows[..., :HD], flat_places)
    fresh_kv = jnp.concatenate([fresh_keys, fresh_rows[..., HD:]], axis=-1).astype(jnp.bfloat16)
    fresh_kv = fresh_kv.reshape(PASSAGES, REC, KVH * 2 * HD)
    queries = jnp.dot(flat_rows, query_weight.reshape(D, QH * HD), preferred_element_type=jnp.float32)
    queries = rotate(queries.reshape(PASSAGES * REC, QH, HD), flat_places) * (HD ** -0.5)
    queries = queries.astype(jnp.bfloat16).reshape(PASSAGES, REC, KVH, group_size, HD)
    blended = jax.vmap(assemble)(cached_pages, page_dest, fresh_kv, rec_rows)
    key_store = blended.reshape(PASSAGES * PASSAGE, KVH, 2 * HD)
    key_rows = key_store[..., :HD].astype(jnp.float32)
    value_rows = key_store[..., HD:].astype(jnp.float32)
    key_places = jnp.arange(PASSAGES * PASSAGE, dtype=jnp.int32)

    def attend_one(bundle):
        passage_queries, passage_places = bundle
        scores = jnp.einsum("rkgd,tkd->kgrt", passage_queries.astype(jnp.float32), key_rows)
        visible = key_places[None, None, None, :] <= passage_places[None, None, :, None]
        scores = jnp.where(visible, scores, masked_score)
        row_max = jnp.max(scores, axis=-1, keepdims=True)
        weights = jnp.exp(scores - row_max)
        weight_sum = jnp.sum(weights, axis=-1)
        rounded = lax.optimization_barrier(weights.astype(jnp.bfloat16)).astype(jnp.float32)
        mixture = jnp.einsum("kgrt,tkd->rkgd", rounded, value_rows)
        mixture = mixture / jnp.transpose(weight_sum, (2, 0, 1))[..., None]
        return mixture.astype(jnp.bfloat16).reshape(REC, KVH, group_size * HD)

    attended = lax.map(attend_one, (queries, places))
    return attended, blended
```

```python
import functools

import jax
import jax.numpy as jnp
import numpy as np
from jax import lax
from jax.experimental import pallas as pl
from jax.experimental.pallas import tpu as pltpu
from jax.sharding import PartitionSpec as P

HD = 128
PASSAGE = 512
PAGE = 16
REC = 128
ROWS = 128
NX, NY = 4, 8
DEPTH = 1024
SLOTS = 16
ROPE_BASE = 500000.0
MASKED = -1e30
QUERY_SCALE = HD**-0.5 * 1.4426950408889634
F32 = jnp.float32
BF16 = jnp.bfloat16
LOGICAL = pl.DeviceIdType.MESH


def wrap(value, count):
    return lax.rem(value, count)


def rotate(values, cosine, signed_sine):
    return values * cosine + pltpu.roll(values, HD // 2, 1) * signed_sine


def kernel(
    hid_hbm, wq_hbm, kvw_hbm, pages_hbm, dest_hbm, rec_hbm, freq_hbm,
    att_hbm, blend_hbm,
    dest_smem, rec_ref, freq_ref, kvw, pages, hall, wall, cont, cont_in, kv_all, v_t,
    q_all, scores, o_out, s_out, o_in, s_in, att,
    local_sem, h_send, h_recv, w_send, w_recv, ws_send, ws_recv,
    c_send, c_recv, kv_send, kv_recv, ks_send, ks_recv,
    q_send, q_recv, o_send, o_recv, s_send, s_recv,
):
    x = lax.axis_index("store")
    sq = lax.axis_index("seq")
    z = lax.axis_index("tp")
    y = sq // 2
    c = wrap(sq, 2)

    def dev(x_to=None, y_to=None, c_to=None, z_to=None):
        x_at = x if x_to is None else x_to
        y_at = y if y_to is None else y_to
        c_at = c if c_to is None else c_to
        z_at = z if z_to is None else z_to
        return (x_at, y_at * 2 + c_at, z_at)

    def remote(src, dst, send_sem, recv_sem, target):
        return pltpu.make_async_remote_copy(
            src_ref=src, dst_ref=dst, send_sem=send_sem, recv_sem=recv_sem,
            device_id=target, device_id_type=LOGICAL,
        )

    def arrived(ref, sem):
        pltpu.make_async_copy(ref, ref, sem).wait()

    sent = []

    def start(copy):
        copy.start()
        sent.append(copy)

    def sent_all():
        for copy in sent:
            copy.wait_send()

    load_hid = pltpu.make_async_copy(hid_hbm, hall.at[x], local_sem.at[0])
    load_kvw = pltpu.make_async_copy(kvw_hbm, kvw, local_sem.at[1])
    load_pages = pltpu.make_async_copy(pages_hbm, pages, local_sem.at[2])
    load_wq = pltpu.make_async_copy(wq_hbm, wall.at[y, c], local_sem.at[3])
    load_dest = pltpu.make_async_copy(dest_hbm, dest_smem, local_sem.at[4])
    load_rec = pltpu.make_async_copy(rec_hbm, rec_ref, local_sem.at[5])
    load_freq = pltpu.make_async_copy(freq_hbm, freq_ref, local_sem.at[6])
    load_rec.start()
    load_freq.start()
    load_hid.start()
    load_kvw.start()
    load_dest.start()
    load_pages.start()
    load_wq.start()

    barrier = pltpu.get_barrier_semaphore()

    def greet(target):
        pl.semaphore_signal(barrier, inc=1, device_id=target, device_id_type=LOGICAL)

    for off in range(1, NX):
        greet(dev(x_to=wrap(x + off, NX)))
    for off in (1, NY - 1):
        greet(dev(y_to=wrap(y + off, NY)))
    greet(dev(c_to=1 - c))

    load_rec.wait()
    load_freq.wait()
    chosen = rec_ref[pl.ds(sq, 1), :]
    row_iota = lax.broadcasted_iota(jnp.int32, (REC, REC), 0)
    lane_iota = lax.broadcasted_iota(jnp.int32, (REC, REC), 1)
    chosen_wide = jnp.broadcast_to(chosen, (REC, REC))
    chosen_col = jnp.sum(
        jnp.where(row_iota == lane_iota, chosen_wide.astype(F32), 0.0), axis=1, keepdims=True
    )
    places = chosen_col + (sq * PASSAGE).astype(F32)
    angles = places * freq_ref[...]
    cosine = jnp.cos(angles)
    sine = jnp.sin(angles)
    signed_sine = jnp.where(lane_iota < HD // 2, -sine, sine)

    load_hid.wait()
    load_kvw.wait()
    fresh = jnp.dot(hall[x], kvw[...], preferred_element_type=F32)
    fresh_keys = rotate(fresh[:, :HD], cosine, signed_sine).astype(BF16)
    fresh_values = fresh[:, HD:].astype(BF16)
    fresh_bf = jnp.concatenate([fresh_keys, fresh_values], axis=1)

    lane_wide = lax.broadcasted_iota(jnp.int32, (1, SLOTS * PAGE), 1)
    target = jnp.full((1, SLOTS * PAGE), -1, jnp.int32)
    load_dest.wait()
    for slot in range(SLOTS):
        page_at = dest_smem[0, slot]
        base = jnp.where(page_at >= 0, page_at * PAGE, -PASSAGE)
        target = jnp.where(lane_wide // PAGE == slot, base + wrap(lane_wide, PAGE), target)
    load_pages.wait()
    for part in range(NX):
        part_rows = lax.broadcasted_iota(jnp.int32, (ROWS, REC), 0) + part * ROWS
        hit = part_rows == chosen_wide
        pick_fresh = jnp.where(hit, 1.0, 0.0)
        keep = 1.0 - jnp.max(pick_fresh, axis=1, keepdims=True)
        wide_rows = lax.broadcasted_iota(jnp.int32, (ROWS, SLOTS * PAGE), 0) + part * ROWS
        pick_page = jnp.where(wide_rows == target, 1.0, 0.0) * keep
        term = jnp.dot(pick_fresh.astype(BF16), fresh_bf, preferred_element_type=F32)
        term = term + jnp.dot(pick_page.astype(BF16), pages[...], preferred_element_type=F32)
        cont[part] = term.astype(BF16)

    pl.semaphore_wait(barrier, 6)

    for off in range(1, NX):
        x_to = wrap(x + off, NX)
        start(
            remote(
                cont.at[x_to], cont_in.at[off - 1], c_send.at[off - 1], c_recv.at[off - 1],
                dev(x_to=x_to),
            )
        )

    right, left, far = wrap(x + 1, NX), wrap(x + NX - 1, NX), wrap(x + 2, NX)
    other = 1 - c
    up, down = dev(y_to=wrap(y + 1, NY)), dev(y_to=wrap(y + NY - 1, NY))

    def half(at):
        return pl.ds(at * DEPTH // 4, DEPTH // 4)

    def weight_below(step):
        return wall.at[wrap(y + NY - step, NY), c]

    def weight_above(step):
        return wall.at[wrap(y + step, NY), c]

    def weight_up(src, block, step, at):
        start(
            remote(
                src.at[half(at)], block.at[half(at)], w_send.at[0, step, at],
                w_recv.at[0, step, at], up,
            )
        )

    def weight_down(src, block, step, at):
        start(
            remote(
                src.at[half(at)], block.at[half(at)], w_send.at[1, step, at],
                w_recv.at[1, step, at], down,
            )
        )

    def weight_core(src, block, step):
        start(remote(src, block, ws_send.at[step], ws_recv.at[step], dev(c_to=other)))

    own = wall.at[y, c]
    weight_up(wq_hbm, own, 0, 0)
    weight_down(wq_hbm, own, 0, 1)
    weight_up(wq_hbm, own, 0, 1)
    weight_down(wq_hbm, own, 0, 0)
    weight_core(wq_hbm, own, 0)

    def weight_relay(step):
        for at in range(2):
            arrived(weight_below(step).at[half(at)], w_recv.at[0, step - 1, at])
            if step < 3 or at == 0:
                weight_up(weight_below(step), weight_below(step), step, at)
            arrived(weight_above(step).at[half(1 - at)], w_recv.at[1, step - 1, 1 - at])
            if step < 3 or at == 0:
                weight_down(weight_above(step), weight_above(step), step, 1 - at)
        weight_core(weight_below(step), weight_below(step), 2 * step - 1)
        weight_core(weight_above(step), weight_above(step), 2 * step)

    def piece(at):
        return pl.ds(at * DEPTH // 2, DEPTH // 2)

    def hidden_right(src, block, step, at):
        start(
            remote(
                src.at[:, piece(at)], block.at[:, piece(at)], h_send.at[0, step],
                h_recv.at[0, step], dev(x_to=right),
            )
        )

    def hidden_left(src, block, step, at):
        start(
            remote(
                src.at[:, piece(at)], block.at[:, piece(at)], h_send.at[1, step],
                h_recv.at[1, step], dev(x_to=left),
            )
        )

    for at in range(4):
        hidden_right(hid_hbm, hall.at[x], at, at)
        hidden_left(hid_hbm, hall.at[x], 3 - at, 3 - at)

    total = cont[x].astype(F32)
    for off in range(1, NX):
        arrived(cont_in.at[off - 1], c_recv.at[off - 1])
        total = total + cont_in[off - 1].astype(F32)
    kv_all[sq] = total.astype(BF16)
    save_blend = pltpu.make_async_copy(kv_all.at[sq], blend_hbm, local_sem.at[0])
    save_blend.start()

    low_rows, high_rows = pl.ds(0, ROWS // 2), pl.ds(ROWS // 2, ROWS // 2)

    def pass_up(block, step):
        start(remote(block, block, kv_send.at[step], kv_recv.at[step], up))

    def pass_down(block, step):
        start(remote(block, block, kv_send.at[4 + step], kv_recv.at[4 + step], down))

    def pass_core(block, step):
        start(remote(block, block, ks_send.at[step], ks_recv.at[step], dev(c_to=other)))

    def below(step):
        return kv_all.at[wrap(y + NY - step, NY) * 2 + c]

    def above(step):
        return kv_all.at[wrap(y + step, NY) * 2 + c]

    def relay(step):
        arrived(below(step), kv_recv.at[step - 1])
        if step < 3:
            pass_up(below(step), step)
        else:
            pass_up(below(step).at[low_rows], step)
        arrived(above(step), kv_recv.at[4 + step - 1])
        if step < 3:
            pass_down(above(step), step)
        else:
            pass_down(above(step).at[high_rows], step)
        pass_core(below(step), 2 * step - 1)
        pass_core(above(step), 2 * step)

    pass_up(kv_all.at[sq], 0)
    pass_down(kv_all.at[sq], 0)
    pass_core(kv_all.at[sq], 0)

    weight_relay(1)
    for at in range(2):
        arrived(hall.at[left, :, piece(at)], h_recv.at[0, at])
        hidden_right(hall.at[left], hall.at[left], 4 + at, at)
        arrived(hall.at[right, :, piece(3 - at)], h_recv.at[1, 3 - at])
        hidden_left(hall.at[right], hall.at[right], 5 - at, 3 - at)

    weight_relay(2)
    relay(1)
    weight_relay(3)
    relay(2)
    relay(3)

    for at in range(2):
        arrived(hall.at[left, :, piece(2 + at)], h_recv.at[0, 2 + at])
        arrived(hall.at[right, :, piece(at)], h_recv.at[1, at])
    for at in range(2):
        arrived(hall.at[far, :, piece(at)], h_recv.at[0, 4 + at])
        arrived(hall.at[far, :, piece(2 + at)], h_recv.at[1, 4 + at])
    load_wq.wait()

    def term(chip):
        lanes = pl.ds(pl.multiple_of(wrap(chip, 2) * DEPTH, DEPTH), DEPTH)
        return jnp.dot(
            hall[chip // 2, :, lanes], wall[chip].reshape(DEPTH, 2 * HD),
            preferred_element_type=F32,
        )

    arrived(wall.at[y, other], ws_recv.at[0])
    q_sum = term(y)
    for step in range(1, 4):
        below_at, above_at = wrap(y + NY - step, NY), wrap(y + step, NY)
        arrived(wall.at[below_at, other], ws_recv.at[2 * step - 1])
        q_sum = q_sum + term(below_at)
        arrived(wall.at[above_at, other], ws_recv.at[2 * step])
        q_sum = q_sum + term(above_at)
    opposite = wrap(y + 4, NY)
    arrived(weight_below(4).at[half(0)], w_recv.at[0, 3, 0])
    arrived(weight_below(4).at[half(1)], w_recv.at[1, 3, 1])
    weight_core(weight_below(4), weight_below(4), 7)
    arrived(wall.at[opposite, other], ws_recv.at[7])
    q_sum = q_sum + term(opposite)

    for head in range(2):
        turned = rotate(q_sum[:, head * HD : (head + 1) * HD], cosine, signed_sine)
        q_all[x, pl.ds(head * REC, REC), :] = (turned * QUERY_SCALE).astype(BF16)
    for off in (2, 1, 3):
        start(
            remote(
                q_all.at[x], q_all.at[x], q_send.at[off], q_recv.at[off],
                dev(x_to=wrap(x + off, NX)),
            )
        )

    arrived(below(4).at[low_rows], kv_recv.at[3])
    arrived(below(4).at[high_rows], kv_recv.at[7])
    pass_core(below(4), 7)
    arrived(kv_all.at[2 * y + other], ks_recv.at[0])
    for step in range(1, 4):
        arrived(kv_all.at[wrap(y + NY - step, NY) * 2 + other], ks_recv.at[2 * step - 1])
        arrived(kv_all.at[wrap(y + step, NY) * 2 + other], ks_recv.at[2 * step])
    arrived(kv_all.at[wrap(y + 4, NY) * 2 + other], ks_recv.at[7])

    def turn(at, carry):
        lanes = pl.ds(pl.multiple_of(at * ROWS, ROWS), ROWS)
        v_t[:, lanes] = kv_all[at, :, HD:].astype(F32).T.astype(BF16)
        return carry

    lax.fori_loop(0, 2 * NY, turn, 0)

    pair = 2 * ROWS
    key_row = lax.broadcasted_iota(jnp.int32, (pair, 2 * REC), 0)
    key_place = (
        (2 * y + key_row // ROWS) * PASSAGE + x * ROWS + wrap(key_row, ROWS)
    )
    query_place = jnp.concatenate([chosen, chosen], axis=1) + sq * PASSAGE

    def attend(off):
        to = wrap(x + off, NX)
        if off:
            arrived(q_all.at[to], q_recv.at[NX - off])
        query = q_all[to]

        def score(at):
            keys = kv_all[pl.ds(2 * at, 2), :, :HD].reshape(pair, HD)
            return lax.dot_general(
                keys, query, (((1,), (1,)), ((), ())), preferred_element_type=F32
            )

        def first(at, top):
            value = score(at)
            scores[at] = value
            return jnp.maximum(top, jnp.max(value.reshape(pair // 8, 8, 2 * REC), axis=0))

        top = lax.fori_loop(0, y, first, jnp.full((8, 2 * REC), MASKED, F32))
        value = jnp.where(key_place <= query_place, score(y), MASKED)
        scores[y] = value
        top = jnp.maximum(top, jnp.max(value.reshape(pair // 8, 8, 2 * REC), axis=0))
        top = jnp.max(top, axis=0, keepdims=True)

        def second(at, carry):
            sums, mixture = carry
            weights = jnp.exp2(scores[at] - top)
            sums = sums + jnp.sum(weights.reshape(pair // 8, 8, 2 * REC), axis=0)
            values = v_t[:, pl.ds(pl.multiple_of(at * pair, pair), pair)]
            mixture = mixture + jnp.dot(
                values, weights.astype(BF16), preferred_element_type=F32
            )
            return sums, mixture

        sums, mixture = lax.fori_loop(
            0, y + 1, second,
            (jnp.zeros((8, 2 * REC), F32), jnp.zeros((HD, 2 * REC), F32)),
        )
        sums = jnp.sum(sums, axis=0, keepdims=True)
        o_out[off] = mixture.astype(BF16)
        s_out[off, 0:1, :] = top
        s_out[off, 1:2, :] = sums
        s_out[off, 2:8, :] = jnp.zeros((6, 2 * REC), F32)
        if off:
            start(
                remote(o_out.at[off], o_in.at[off], o_send.at[off], o_recv.at[off], dev(x_to=to))
            )
            start(
                remote(s_out.at[off], s_in.at[off], s_send.at[off], s_recv.at[off], dev(x_to=to))
            )

    attend(0)
    attend(1)
    attend(3)
    attend(2)

    for off in (1, 3, 2):
        arrived(o_in.at[off], o_recv.at[off])
        arrived(s_in.at[off], s_recv.at[off])
    s_in[0] = s_out[0]
    o_in[0] = o_out[0]
    tops = [s_in[off, 0:1, :] for off in range(NX)]
    parts = [s_in[off, 1:2, :] for off in range(NX)]
    top = jnp.maximum(jnp.maximum(tops[0], tops[1]), jnp.maximum(tops[2], tops[3]))
    factors = [jnp.exp2(value - top) for value in tops]
    whole = sum(part * factor for part, factor in zip(parts, factors))
    mixed = sum(o_in[off].astype(F32) * factors[off] for off in range(NX))
    mixed = mixed / whole
    for head in range(2):
        att[:, head * HD : (head + 1) * HD] = (
            mixed[:, head * REC : (head + 1) * REC].T.astype(BF16)
        )
    save_att = pltpu.make_async_copy(att, att_hbm, local_sem.at[1])
    save_att.start()

    sent_all()
    save_blend.wait()
    save_att.wait()


def on_device(hidden_rows, query_weight, kv_weight, cached_pages, page_dest, rec_rows):
    half = np.arange(HD) % (HD // 2)
    frequency = np.asarray(ROPE_BASE ** (-(half * 2.0 / HD)), np.float32).reshape(1, HD)
    depth = query_weight.shape[0]
    dma = pltpu.SemaphoreType.DMA
    hbm = pl.BlockSpec(memory_space=pltpu.HBM)
    attended, blended = pl.pallas_call(
        kernel,
        out_shape=(
            jax.ShapeDtypeStruct((REC, 2 * HD), BF16),
            jax.ShapeDtypeStruct((ROWS, 2 * HD), BF16),
        ),
        in_specs=[hbm] * 7,
        out_specs=(hbm, hbm),
        scratch_shapes=[
            pltpu.SMEM((1, SLOTS), jnp.int32),
            pltpu.VMEM((2 * NY, REC), jnp.int32),
            pltpu.VMEM((1, HD), F32),
            pltpu.VMEM((2 * DEPTH, 2 * HD), BF16),
            pltpu.VMEM((SLOTS * PAGE, 2 * HD), BF16),
            pltpu.VMEM((NX, REC, 2 * DEPTH), BF16),
            pltpu.VMEM((NY, 2, DEPTH // 2, 2 * HD), BF16),
            pltpu.VMEM((NX, ROWS, 2 * HD), BF16),
            pltpu.VMEM((NX - 1, ROWS, 2 * HD), BF16),
            pltpu.VMEM((2 * NY, ROWS, 2 * HD), BF16),
            pltpu.VMEM((HD, 2 * NY * ROWS), BF16),
            pltpu.VMEM((NX, 2 * REC, HD), BF16),
            pltpu.VMEM((NY, 2 * ROWS, 2 * REC), F32),
            pltpu.VMEM((NX, HD, 2 * REC), BF16),
            pltpu.VMEM((NX, 8, 2 * REC), F32),
            pltpu.VMEM((NX, HD, 2 * REC), BF16),
            pltpu.VMEM((NX, 8, 2 * REC), F32),
            pltpu.VMEM((REC, 2 * HD), BF16),
            dma((7,)),
            dma((2, 6)), dma((2, 6)),
            dma((2, 4, 2)), dma((2, 4, 2)),
            dma((8,)), dma((8,)),
            dma((3,)), dma((3,)),
            dma((8,)), dma((8,)),
            dma((8,)), dma((8,)),
            dma((NX,)), dma((NX,)),
            dma((NX,)), dma((NX,)),
            dma((NX,)), dma((NX,)),
        ],
        compiler_params=pltpu.CompilerParams(
            collective_id=0, has_side_effects=True, vmem_limit_bytes=64 * 1024 * 1024
        ),
    )(
        hidden_rows.reshape(REC, -1),
        query_weight.reshape(depth, 2 * HD),
        kv_weight,
        cached_pages.reshape(SLOTS * PAGE, 2 * HD),
        page_dest,
        rec_rows,
        jnp.asarray(frequency),
    )
    return attended.reshape(1, REC, 1, 2 * HD), blended.reshape(1, ROWS, 2 * HD)


def solution(mesh):
    placed = (
        P("seq", None, "store"),
        P("seq", "tp", "store"),
        P("store", "tp"),
        P("seq", "store", None, "tp"),
        P("seq", "store"),
        P(),
    )
    return jax.shard_map(
        on_device,
        mesh=mesh,
        in_specs=placed,
        out_specs=(P("seq", None, "tp", "store"), P("seq", "store", "tp")),
        check_vma=False,
    )
```

```python
import functools

import jax
import jax.numpy as jnp
import numpy as np
from jax import lax
from jax.experimental import pallas as pl
from jax.experimental.pallas import tpu as pltpu
from jax.sharding import PartitionSpec as P

HD = 128
PASSAGE = 512
PAGE = 16
REC = 128
ROWS = 128
NX, NY = 4, 8
DEPTH = 1024
SLOTS = 16
ROPE_BASE = 500000.0
MASKED = -1e30
QUERY_SCALE = HD**-0.5 * 1.4426950408889634
F32 = jnp.float32
BF16 = jnp.bfloat16
LOGICAL = pl.DeviceIdType.MESH


def wrap(value, count):
    return lax.rem(value, count)


def rotate(values, cosine, signed_sine):
    return values * cosine + pltpu.roll(values, HD // 2, 1) * signed_sine


def kernel(
    hid_hbm, wq_hbm, kvw_hbm, pages_hbm, dest_hbm, rec_hbm, freq_hbm,
    att_hbm, blend_hbm,
    dest_smem, rec_ref, freq_ref, kvw, pages, hall, wall, cont, cont_in, kv_all, v_t,
    q_all, scores, probs, o_out, s_out, o_in, s_in, att,
    local_sem, h_send, h_recv, w_send, w_recv, ws_send, ws_recv,
    c_send, c_recv, kv_send, kv_recv, ks_send, ks_recv,
    q_send, q_recv, o_send, o_recv, s_send, s_recv,
):
    x = lax.axis_index("store")
    sq = lax.axis_index("seq")
    z = lax.axis_index("tp")
    y = sq // 2
    c = wrap(sq, 2)

    def dev(x_to=None, y_to=None, c_to=None, z_to=None):
        x_at = x if x_to is None else x_to
        y_at = y if y_to is None else y_to
        c_at = c if c_to is None else c_to
        z_at = z if z_to is None else z_to
        return (x_at, y_at * 2 + c_at, z_at)

    def remote(src, dst, send_sem, recv_sem, target):
        return pltpu.make_async_remote_copy(
            src_ref=src, dst_ref=dst, send_sem=send_sem, recv_sem=recv_sem,
            device_id=target, device_id_type=LOGICAL,
        )

    def arrived(ref, sem):
        pltpu.make_async_copy(ref, ref, sem).wait()

    sent = []

    def start(copy):
        copy.start()
        sent.append(copy)

    def sent_all():
        for copy in sent:
            copy.wait_send()

    load_hid = pltpu.make_async_copy(hid_hbm, hall.at[x], local_sem.at[0])
    load_kvw = pltpu.make_async_copy(kvw_hbm, kvw, local_sem.at[1])
    load_pages = pltpu.make_async_copy(pages_hbm, pages, local_sem.at[2])
    load_wq = pltpu.make_async_copy(wq_hbm, wall.at[y, c], local_sem.at[3])
    load_dest = pltpu.make_async_copy(dest_hbm, dest_smem, local_sem.at[4])
    load_rec = pltpu.make_async_copy(rec_hbm, rec_ref, local_sem.at[5])
    load_freq = pltpu.make_async_copy(freq_hbm, freq_ref, local_sem.at[6])
    load_rec.start()
    load_freq.start()
    load_hid.start()
    load_kvw.start()
    load_dest.start()
    load_pages.start()
    load_wq.start()

    barrier = pltpu.get_barrier_semaphore()

    def greet(target):
        pl.semaphore_signal(barrier, inc=1, device_id=target, device_id_type=LOGICAL)

    for off in range(1, NX):
        greet(dev(x_to=wrap(x + off, NX)))
    for off in (1, NY - 1):
        greet(dev(y_to=wrap(y + off, NY)))
    greet(dev(c_to=1 - c))

    pl.semaphore_wait(barrier, 6)

    right, left, far = wrap(x + 1, NX), wrap(x + NX - 1, NX), wrap(x + 2, NX)
    other = 1 - c
    up, down = dev(y_to=wrap(y + 1, NY)), dev(y_to=wrap(y + NY - 1, NY))

    def half(at):
        return pl.ds(at * DEPTH // 4, DEPTH // 4)

    def weight_below(step):
        return wall.at[wrap(y + NY - step, NY), c]

    def weight_above(step):
        return wall.at[wrap(y + step, NY), c]

    def weight_up(src, block, step, at):
        start(
            remote(
                src.at[half(at)], block.at[half(at)], w_send.at[0, step, at],
                w_recv.at[0, step, at], up,
            )
        )

    def weight_down(src, block, step, at):
        start(
            remote(
                src.at[half(at)], block.at[half(at)], w_send.at[1, step, at],
                w_recv.at[1, step, at], down,
            )
        )

    def weight_core(src, block, step):
        start(remote(src, block, ws_send.at[step], ws_recv.at[step], dev(c_to=other)))

    own = wall.at[y, c]
    weight_up(wq_hbm, own, 0, 0)
    weight_down(wq_hbm, own, 0, 1)
    weight_up(wq_hbm, own, 0, 1)
    weight_down(wq_hbm, own, 0, 0)
    weight_core(wq_hbm, own, 0)

    def weight_relay(step, at):
        arrived(weight_below(step).at[half(at)], w_recv.at[0, step - 1, at])
        if step < 3 or at == 0:
            weight_up(weight_below(step), weight_below(step), step, at)
        arrived(weight_above(step).at[half(1 - at)], w_recv.at[1, step - 1, 1 - at])
        if step < 3 or at == 0:
            weight_down(weight_above(step), weight_above(step), step, 1 - at)
        if at == 1:
            weight_core(weight_below(step), weight_below(step), 2 * step - 1)
            weight_core(weight_above(step), weight_above(step), 2 * step)

    def piece(at):
        return pl.ds(at * DEPTH // 2, DEPTH // 2)

    def hidden_right(src, block, step, at):
        start(
            remote(
                src.at[:, piece(at)], block.at[:, piece(at)], h_send.at[0, step],
                h_recv.at[0, step], dev(x_to=right),
            )
        )

    def hidden_left(src, block, step, at):
        start(
            remote(
                src.at[:, piece(at)], block.at[:, piece(at)], h_send.at[1, step],
                h_recv.at[1, step], dev(x_to=left),
            )
        )

    load_rec.wait()
    load_freq.wait()
    chosen = rec_ref[pl.ds(sq, 1), :]
    row_iota = lax.broadcasted_iota(jnp.int32, (REC, REC), 0)
    lane_iota = lax.broadcasted_iota(jnp.int32, (REC, REC), 1)
    chosen_wide = jnp.broadcast_to(chosen, (REC, REC))
    chosen_col = jnp.sum(
        jnp.where(row_iota == lane_iota, chosen_wide.astype(F32), 0.0), axis=1, keepdims=True
    )
    places = chosen_col + (sq * PASSAGE).astype(F32)
    angles = places * freq_ref[...]
    cosine = jnp.cos(angles)
    sine = jnp.sin(angles)
    signed_sine = jnp.where(lane_iota < HD // 2, -sine, sine)

    load_hid.wait()
    load_kvw.wait()
    fresh = jnp.dot(hall[x], kvw[...], preferred_element_type=F32)
    fresh_keys = rotate(fresh[:, :HD], cosine, signed_sine).astype(BF16)
    fresh_values = fresh[:, HD:].astype(BF16)
    fresh_bf = jnp.concatenate([fresh_keys, fresh_values], axis=1)

    lane_wide = lax.broadcasted_iota(jnp.int32, (1, SLOTS * PAGE), 1)
    target = jnp.full((1, SLOTS * PAGE), -1, jnp.int32)
    load_dest.wait()
    for slot in range(SLOTS):
        page_at = dest_smem[0, slot]
        base = jnp.where(page_at >= 0, page_at * PAGE, -PASSAGE)
        target = jnp.where(lane_wide // PAGE == slot, base + wrap(lane_wide, PAGE), target)
    load_pages.wait()
    for part in range(NX):
        part_rows = lax.broadcasted_iota(jnp.int32, (ROWS, REC), 0) + part * ROWS
        hit = part_rows == chosen_wide
        pick_fresh = jnp.where(hit, 1.0, 0.0)
        keep = 1.0 - jnp.max(pick_fresh, axis=1, keepdims=True)
        wide_rows = lax.broadcasted_iota(jnp.int32, (ROWS, SLOTS * PAGE), 0) + part * ROWS
        pick_page = jnp.where(wide_rows == target, 1.0, 0.0) * keep
        term = jnp.dot(pick_fresh.astype(BF16), fresh_bf, preferred_element_type=F32)
        term = term + jnp.dot(pick_page.astype(BF16), pages[...], preferred_element_type=F32)
        cont[part] = term.astype(BF16)

    for off in range(1, NX):
        x_to = wrap(x + off, NX)
        start(
            remote(
                cont.at[x_to], cont_in.at[off - 1], c_send.at[off - 1], c_recv.at[off - 1],
                dev(x_to=x_to),
            )
        )

    for at in range(4):
        hidden_right(hid_hbm, hall.at[x], at, at)
        hidden_left(hid_hbm, hall.at[x], 3 - at, 3 - at)

    weight_relay(1, 0)
    weight_relay(1, 1)

    total = cont[x].astype(F32)
    for off in range(1, NX):
        arrived(cont_in.at[off - 1], c_recv.at[off - 1])
        total = total + cont_in[off - 1].astype(F32)
    kv_all[sq] = total.astype(BF16)
    save_blend = pltpu.make_async_copy(kv_all.at[sq], blend_hbm, local_sem.at[0])
    save_blend.start()

    low_rows, high_rows = pl.ds(0, ROWS // 2), pl.ds(ROWS // 2, ROWS // 2)

    def pass_up(block, step):
        start(remote(block, block, kv_send.at[step], kv_recv.at[step], up))

    def pass_down(block, step):
        start(remote(block, block, kv_send.at[4 + step], kv_recv.at[4 + step], down))

    def pass_core(block, step):
        start(remote(block, block, ks_send.at[step], ks_recv.at[step], dev(c_to=other)))

    def below(step):
        return kv_all.at[wrap(y + NY - step, NY) * 2 + c]

    def above(step):
        return kv_all.at[wrap(y + step, NY) * 2 + c]

    def relay(step):
        arrived(below(step), kv_recv.at[step - 1])
        if step < 3:
            pass_up(below(step), step)
        else:
            pass_up(below(step).at[low_rows], step)
        arrived(above(step), kv_recv.at[4 + step - 1])
        if step < 3:
            pass_down(above(step), step)
        else:
            pass_down(above(step).at[high_rows], step)
        pass_core(below(step), 2 * step - 1)
        pass_core(above(step), 2 * step)

    pass_up(kv_all.at[sq], 0)
    pass_down(kv_all.at[sq], 0)
    pass_core(kv_all.at[sq], 0)

    def hidden_relay(at):
        arrived(hall.at[left, :, piece(at)], h_recv.at[0, at])
        hidden_right(hall.at[left], hall.at[left], 4 + at, at)
        arrived(hall.at[right, :, piece(3 - at)], h_recv.at[1, 3 - at])
        hidden_left(hall.at[right], hall.at[right], 5 - at, 3 - at)

    weight_relay(2, 0)
    hidden_relay(0)
    weight_relay(2, 1)
    relay(1)
    hidden_relay(1)
    weight_relay(3, 0)
    relay(2)
    weight_relay(3, 1)

    for at in range(2):
        arrived(hall.at[left, :, piece(2 + at)], h_recv.at[0, 2 + at])
        arrived(hall.at[right, :, piece(at)], h_recv.at[1, at])
    for at in range(2):
        arrived(hall.at[far, :, piece(at)], h_recv.at[0, 4 + at])
        arrived(hall.at[far, :, piece(2 + at)], h_recv.at[1, 4 + at])
    load_wq.wait()

    def term(chip):
        lanes = pl.ds(pl.multiple_of(wrap(chip, 2) * DEPTH, DEPTH), DEPTH)
        return jnp.dot(
            hall[chip // 2, :, lanes], wall[chip].reshape(DEPTH, 2 * HD),
            preferred_element_type=F32,
        )

    arrived(wall.at[y, other], ws_recv.at[0])
    q_sum = term(y)
    for step in range(1, 4):
        below_at, above_at = wrap(y + NY - step, NY), wrap(y + step, NY)
        arrived(wall.at[below_at, other], ws_recv.at[2 * step - 1])
        q_sum = q_sum + term(below_at)
        arrived(wall.at[above_at, other], ws_recv.at[2 * step])
        q_sum = q_sum + term(above_at)
    opposite = wrap(y + 4, NY)
    relay(3)
    arrived(weight_below(4).at[half(0)], w_recv.at[0, 3, 0])
    arrived(weight_below(4).at[half(1)], w_recv.at[1, 3, 1])
    weight_core(weight_below(4), weight_below(4), 7)
    arrived(wall.at[opposite, other], ws_recv.at[7])
    q_sum = q_sum + term(opposite)

    for head in range(2):
        turned = rotate(q_sum[:, head * HD : (head + 1) * HD], cosine, signed_sine)
        q_all[x, pl.ds(head * REC, REC), :] = (turned * QUERY_SCALE).astype(BF16)
    for off in (2, 1, 3):
        start(
            remote(
                q_all.at[x], q_all.at[x], q_send.at[off], q_recv.at[off],
                dev(x_to=wrap(x + off, NX)),
            )
        )

    arrived(below(4).at[low_rows], kv_recv.at[3])
    arrived(below(4).at[high_rows], kv_recv.at[7])
    pass_core(below(4), 7)
    arrived(kv_all.at[2 * y + other], ks_recv.at[0])
    for step in range(1, 4):
        arrived(kv_all.at[wrap(y + NY - step, NY) * 2 + other], ks_recv.at[2 * step - 1])
        arrived(kv_all.at[wrap(y + step, NY) * 2 + other], ks_recv.at[2 * step])
    arrived(kv_all.at[wrap(y + 4, NY) * 2 + other], ks_recv.at[7])

    def turn(at, carry):
        lanes = pl.ds(pl.multiple_of(at * ROWS, ROWS), ROWS)
        v_t[:, lanes] = kv_all[at, :, HD:].astype(F32).T.astype(BF16)
        return carry

    lax.fori_loop(0, 2 * NY, turn, 0)

    pair = 2 * ROWS
    key_row = lax.broadcasted_iota(jnp.int32, (pair, 2 * REC), 0)
    key_place = key_row // ROWS * PASSAGE + x * ROWS + wrap(key_row, ROWS)
    query_place = jnp.concatenate([chosen, chosen], axis=1) + sq * PASSAGE

    def attend(off):
        to = wrap(x + off, NX)
        if off:
            arrived(q_all.at[to], q_recv.at[NX - off])
        query = q_all[to]

        top = jnp.full((8, 2 * REC), MASKED, F32)
        for at in range(NY):
            keys = kv_all[2 * at : 2 * at + 2, :, :HD].reshape(pair, HD)
            value = lax.dot_general(
                keys, query, (((1,), (1,)), ((), ())), preferred_element_type=F32
            )
            value = jnp.where(key_place + 2 * at * PASSAGE <= query_place, value, MASKED)
            scores[at] = value
            top = jnp.maximum(top, jnp.max(value.reshape(pair // 8, 8, 2 * REC), axis=0))
        top = jnp.max(top, axis=0, keepdims=True)
        sums = jnp.zeros((8, 2 * REC), F32)
        for at in range(NY):
            weights = jnp.exp2(scores[at] - top)
            sums = sums + jnp.sum(weights.reshape(pair // 8, 8, 2 * REC), axis=0)
            probs[at * pair : (at + 1) * pair] = weights.astype(BF16)
        sums = jnp.sum(sums, axis=0, keepdims=True)
        mixture = jnp.dot(v_t[...], probs[...], preferred_element_type=F32)
        o_out[off] = mixture.astype(BF16)
        s_out[off, 0:1, :] = top
        s_out[off, 1:2, :] = sums
        s_out[off, 2:8, :] = jnp.zeros((6, 2 * REC), F32)
        if off:
            start(
                remote(o_out.at[off], o_in.at[off], o_send.at[off], o_recv.at[off], dev(x_to=to))
            )
            start(
                remote(s_out.at[off], s_in.at[off], s_send.at[off], s_recv.at[off], dev(x_to=to))
            )

    attend(0)
    attend(2)
    attend(1)
    attend(3)

    for off in (1, 3, 2):
        arrived(o_in.at[off], o_recv.at[off])
        arrived(s_in.at[off], s_recv.at[off])
    s_in[0] = s_out[0]
    o_in[0] = o_out[0]
    tops = [s_in[off, 0:1, :] for off in range(NX)]
    parts = [s_in[off, 1:2, :] for off in range(NX)]
    top = jnp.maximum(jnp.maximum(tops[0], tops[1]), jnp.maximum(tops[2], tops[3]))
    factors = [jnp.exp2(value - top) for value in tops]
    whole = sum(part * factor for part, factor in zip(parts, factors))
    mixed = sum(o_in[off].astype(F32) * factors[off] for off in range(NX))
    mixed = mixed / whole
    for head in range(2):
        att[:, head * HD : (head + 1) * HD] = (
            mixed[:, head * REC : (head + 1) * REC].T.astype(BF16)
        )
    save_att = pltpu.make_async_copy(att, att_hbm, local_sem.at[1])
    save_att.start()

    sent_all()
    save_blend.wait()
    save_att.wait()


def on_device(hidden_rows, query_weight, kv_weight, cached_pages, page_dest, rec_rows):
    half = np.arange(HD) % (HD // 2)
    frequency = np.asarray(ROPE_BASE ** (-(half * 2.0 / HD)), np.float32).reshape(1, HD)
    depth = query_weight.shape[0]
    dma = pltpu.SemaphoreType.DMA
    hbm = pl.BlockSpec(memory_space=pltpu.HBM)
    attended, blended = pl.pallas_call(
        kernel,
        out_shape=(
            jax.ShapeDtypeStruct((REC, 2 * HD), BF16),
            jax.ShapeDtypeStruct((ROWS, 2 * HD), BF16),
        ),
        in_specs=[hbm] * 7,
        out_specs=(hbm, hbm),
        scratch_shapes=[
            pltpu.SMEM((1, SLOTS), jnp.int32),
            pltpu.VMEM((2 * NY, REC), jnp.int32),
            pltpu.VMEM((1, HD), F32),
            pltpu.VMEM((2 * DEPTH, 2 * HD), BF16),
            pltpu.VMEM((SLOTS * PAGE, 2 * HD), BF16),
            pltpu.VMEM((NX, REC, 2 * DEPTH), BF16),
            pltpu.VMEM((NY, 2, DEPTH // 2, 2 * HD), BF16),
            pltpu.VMEM((NX, ROWS, 2 * HD), BF16),
            pltpu.VMEM((NX - 1, ROWS, 2 * HD), BF16),
            pltpu.VMEM((2 * NY, ROWS, 2 * HD), BF16),
            pltpu.VMEM((HD, 2 * NY * ROWS), BF16),
            pltpu.VMEM((NX, 2 * REC, HD), BF16),
            pltpu.VMEM((NY, 2 * ROWS, 2 * REC), F32),
            pltpu.VMEM((2 * NY * ROWS, 2 * REC), BF16),
            pltpu.VMEM((NX, HD, 2 * REC), BF16),
            pltpu.VMEM((NX, 8, 2 * REC), F32),
            pltpu.VMEM((NX, HD, 2 * REC), BF16),
            pltpu.VMEM((NX, 8, 2 * REC), F32),
            pltpu.VMEM((REC, 2 * HD), BF16),
            dma((7,)),
            dma((2, 6)), dma((2, 6)),
            dma((2, 4, 2)), dma((2, 4, 2)),
            dma((8,)), dma((8,)),
            dma((3,)), dma((3,)),
            dma((8,)), dma((8,)),
            dma((8,)), dma((8,)),
            dma((NX,)), dma((NX,)),
            dma((NX,)), dma((NX,)),
            dma((NX,)), dma((NX,)),
        ],
        compiler_params=pltpu.CompilerParams(
            collective_id=0, has_side_effects=True, vmem_limit_bytes=64 * 1024 * 1024
        ),
    )(
        hidden_rows.reshape(REC, -1),
        query_weight.reshape(depth, 2 * HD),
        kv_weight,
        cached_pages.reshape(SLOTS * PAGE, 2 * HD),
        page_dest,
        rec_rows,
        jnp.asarray(frequency),
    )
    return attended.reshape(1, REC, 1, 2 * HD), blended.reshape(1, ROWS, 2 * HD)


def solution(mesh):
    placed = (
        P("seq", None, "store"),
        P("seq", "tp", "store"),
        P("store", "tp"),
        P("seq", "store", None, "tp"),
        P("seq", "store"),
        P(),
    )
    return jax.shard_map(
        on_device,
        mesh=mesh,
        in_specs=placed,
        out_specs=(P("seq", None, "tp", "store"), P("seq", "store", "tp")),
        check_vma=False,
    )
```
